1024 devices in a mesh: blk: 64 (over z, core), rep: 16 (over x, y).
Axes of the slice: x: 4, y: 4, z: 32, core: 2. Of those that a mesh axis runs over, the one named last changes fastest.
Arguments:
- t_slab: bfloat16 [16, 1024, 64, 1024], P('rep', 'blk'), may hold values from -12 to 12
- w_cycle: bfloat16 [16, 1, 1024, 1024], P('rep'), may hold values from -0.75 to 0.75
- k_irrep: int32 [16], P('rep'), may hold values from 0 to 7
- i_irrep: int32 [64], replicated, may hold values from 0 to 7, as said below
- j_irrep: int32 [1], replicated, may hold values from 0 to 7
- tile_irrep: int32 [8], replicated, may hold values from 0 to 7, each once
- i_energy: float32 [64], replicated, may hold values from -2.5 to -0.5
- j_energy: float32 [1], replicated, may hold values from -2.5 to -0.5
- vir_energy: float32 [1024], replicated, may hold values from 0.3 to 3
Outputs:
- amplitude_update: float32 [1, 64, 1024, 1024], P(None, None, 'blk', 'rep')
The draws below stay inside these ranges and needn't reach their ends.
Inputs may be any that keep to these rules, and one draw needn't show every extreme that they name: tile_irrep holds each of the 8 irreps exactly once. The orbitals i come in 8 runs of 8 consecutive orbitals; i_irrep is the same within a run, and each irrep labels exactly one run.
All inputs are finite; a program needn't handle non-finite values.
Results may differ from the reference program's by a relative error of at most 0.0003.
Values may be sent and summed in bfloat16 or wider, within the bound.
A program may use at most 32 MiB of HBM per device.

```python
import jax
import jax.numpy as jnp
from jax import lax

TILE = 128
VP = 1024
NJ = 1
NI = 64
NK = 16


def draw_i_irrep(key, part):
    key = jax.random.fold_in(key, 11)
    order = jax.random.permutation(key, jnp.arange(8, dtype=jnp.int32))
    runs = jnp.arange(NI, dtype=jnp.int32) // (NI // 8)
    return order[runs].astype(jnp.int32)


def with_ends(drawn, stream_key, least, top_value):
    spot = [jax.random.randint(jax.random.fold_in(stream_key, axis), (), 0, length) for axis, length in enumerate(drawn.shape)]
    main_axis = drawn.shape.index(max(drawn.shape))
    neighbour = spot[:main_axis] + [(spot[main_axis] + 1) % drawn.shape[main_axis]] + spot[main_axis + 1:]
    return drawn.at[tuple(spot)].set(least).at[tuple(neighbour)].set(top_value)


def raised(values, key, source, target, blocks, factor):
    def block_of(position):
        return (jnp.arange(values.shape[position]) // (values.shape[position] // blocks)).reshape((-1,) + (1,) * (values.ndim - 1 - position))

    one_side = jax.random.permutation(key, blocks)[block_of(target)]
    second = (block_of(target) + blocks // 2) % blocks
    return jnp.where((block_of(source) == one_side) | (block_of(source) == second), factor * values, values)


def steps_of(own_key, shape, shards, low, high):
    gain = 1.0
    for position, parts in shards:
        heights = jax.random.uniform(jax.random.fold_in(jax.random.fold_in(own_key, 6), position), (parts,), jnp.float32, low / len(shards), high / len(shards))
        gain = gain * jnp.repeat(jnp.exp(heights), shape[position] // parts).reshape((-1,) + (1,) * (len(shape) - 1 - position))
    return gain


def bell_draw(key, shape, deviation, bound, cuts=(), held_as=jnp.bfloat16):
    values = jax.random.normal(key, shape, jnp.float32) * deviation
    if len(cuts) > 0:
        values = steps_of(key, shape, cuts, -0.22, 0.18) * values
    return jnp.clip(values, min=-bound, max=bound).astype(held_as)


def bell_draw_with(own_key, shape, spread, bound, cuts, heavy, held_as=jnp.bfloat16):
    drawn = spread * jax.random.normal(own_key, shape, jnp.float32)
    if cuts:
        drawn = drawn * steps_of(own_key, shape, cuts, -0.22, 0.18)
    return jnp.clip(raised(drawn, jax.random.fold_in(own_key, 3), *heavy), -bound, bound).astype(held_as)


def setup_inputs(seed: int = 0) -> dict:
    streams_of = jax.random.split(jax.random.key(seed), 10)
    return {
        "t_slab": bell_draw(streams_of[0], (NK, VP, NI, VP), 2.0, 12.0, ((0, 16), (1, 64))),
        "w_cycle": bell_draw_with(streams_of[1], (NK, NJ, VP, VP), TILE ** -0.5, 0.75, ((0, 16),), (0, 3, 16, 2.0)),
        "k_irrep": with_ends(jax.random.randint(streams_of[2], (NK,), 0, 8), jax.random.fold_in(streams_of[2], 1), 0, 7).astype(jnp.int32),
        "i_irrep": draw_i_irrep(jax.random.fold_in(streams_of[9], 71), 0),
        "j_irrep": jax.random.randint(streams_of[4], (NJ,), 0, 8).astype(jnp.int32),
        "tile_irrep": jax.random.permutation(streams_of[5], 8).astype(jnp.int32),
        "i_energy": jnp.clip(jax.random.uniform(streams_of[6], (NI,), jnp.float32, -2.5, -0.5), -2.5, -0.5),
        "j_energy": jnp.clip(jax.random.uniform(streams_of[7], (NJ,), jnp.float32, -2.5, -0.5), -2.5, -0.5),
        "vir_energy": jnp.clip(jax.random.uniform(streams_of[8], (VP,), jnp.float32, 0.3, 3.0), 0.3, 3.0),
    }


def reference(t_slab, w_cycle, k_irrep, i_irrep, j_irrep, tile_irrep, i_energy, j_energy, vir_energy):
    vir_irrep = jnp.repeat(tile_irrep, TILE)

    def step(total, pieces):
        amp, cycle_w, k_label = pieces
        mask_amp = jnp.bitwise_xor(jnp.bitwise_xor(k_label, vir_irrep[:, None, None]), jnp.bitwise_xor(i_irrep[None, :, None], vir_irrep[None, None, :])) == 0
        mask_cycle = jnp.bitwise_xor(jnp.bitwise_xor(k_label, j_irrep[:, None, None]), jnp.bitwise_xor(vir_irrep[None, :, None], vir_irrep[None, None, :])) == 0
        left = jnp.where(mask_amp, amp.astype(jnp.float32), jnp.zeros((), jnp.float32))
        right = jnp.where(mask_cycle, cycle_w.astype(jnp.float32), jnp.zeros((), jnp.float32))
        total = total + lax.dot_general(left, right, (((0,), (1,)), ((), ())), precision=lax.Precision.HIGHEST)
        return total, None

    start = jnp.zeros((NI, VP, NJ, VP), jnp.float32)
    cycle, unused = lax.scan(step, start, (t_slab, w_cycle, k_irrep))
    cycle = jnp.transpose(cycle, (2, 0, 1, 3))
    denom = vir_energy[None, None, :, None] + vir_energy[None, None, None, :] - i_energy[None, :, None, None] - j_energy[:, None, None, None]
    return cycle / denom
```

```python
import functools

import jax
import jax.numpy as jnp
from jax import lax
from jax.experimental import pallas as pl
from jax.experimental.pallas import tpu as pltpu
from jax.sharding import PartitionSpec as P

TILE = 128
RUNS = 8
MESH = pl.DeviceIdType.MESH


def pick(position, scalars):
    label = jnp.zeros(position.shape, jnp.int32)
    for place, scalar in enumerate(scalars):
        label = jnp.where(position == place, scalar, label)
    return label


def swap_blocks(rows, width):
    count = len(rows)
    block = lax.broadcasted_iota(jnp.int32, rows[0].shape, 1) // width
    step = count // 2
    while step:
        low = (block // step) % 2 == 0
        new = list(rows)
        for i in range(count):
            if i & step == 0:
                j = i | step
                new[i] = jnp.where(low, rows[i], pltpu.roll(rows[j], step * width, 1))
                new[j] = jnp.where(low, pltpu.roll(rows[i], TILE - step * width, 1), rows[j])
        rows = new
        step //= 2
    return rows


def kernel(
    blk_count,
    rep_count,
    k_ref,
    i_ref,
    j_ref,
    tile_ref,
    t_hbm,
    w_hbm,
    out_ref,
    t_vm,
    w_vm,
    x_vm,
    wt_vm,
    send,
    recv,
    part_send,
    part_recv,
    local_sem,
    send_sem,
    recv_sem,
    part_send_sem,
    part_recv_sem,
):
    c_width, rows_i, full = t_vm.shape
    tiles = full // TILE
    run_len = rows_i // RUNS
    group = blk_count // tiles
    a_width = full // blk_count
    b_width = full // rep_count
    chips = blk_count // 2
    me_p = lax.axis_index("blk")
    me_r = lax.axis_index("rep")

    t_copy = pltpu.make_async_copy(t_hbm, t_vm, local_sem.at[0])
    t_copy.start()
    w_copy = pltpu.make_async_copy(w_hbm, w_vm, local_sem.at[1])
    w_copy.start()

    barrier = pltpu.get_barrier_semaphore()

    def greet_blk(step, carry):
        other = lax.rem(me_p + step, blk_count)
        pl.semaphore_signal(barrier, inc=1, device_id={"blk": other}, device_id_type=MESH)
        return carry

    def greet_rep(step, carry):
        other = lax.rem(me_r + step, rep_count)
        pl.semaphore_signal(barrier, inc=1, device_id={"rep": other}, device_id_type=MESH)
        return carry

    lax.fori_loop(1, blk_count, greet_blk, 0)
    lax.fori_loop(1, rep_count, greet_rep, 0)

    irreps = [tile_ref[t] for t in range(tiles)]
    c_irrep = tile_ref[me_p // group]
    row = lax.broadcasted_iota(jnp.int32, (rows_i, full), 0)
    col = lax.broadcasted_iota(jnp.int32, (rows_i, full), 1)
    run_label = pick(row // run_len, [i_ref[g * run_len] for g in range(RUNS)])
    a_label = pick(col // TILE, irreps)
    keep = (run_label ^ a_label) == (k_ref[0] ^ c_irrep)
    mask = jnp.where(keep, 1.0, 0.0).astype(jnp.bfloat16)
    row = lax.broadcasted_iota(jnp.int32, (run_len * c_width, 16 * c_width), 0)
    col = lax.broadcasted_iota(jnp.int32, (run_len * c_width, 16 * c_width), 1)
    chosen = (row % c_width == col // 16) & (row // c_width == col % run_len)
    order = jnp.where(chosen, 1.0, 0.0).astype(jnp.bfloat16)

    t_copy.wait()
    kept = []
    for c in range(c_width):
        held = t_vm[c] * mask
        kept.append(sum(held[16 * q : 16 * q + 16] for q in range(rows_i // 16)))
    kept = jnp.concatenate(kept, axis=0)
    x_vm[...] = jnp.dot(order, kept, preferred_element_type=jnp.float32)
    for t in range(tiles):
        blocks = [
            x_vm[i * c_width : (i + 1) * c_width, t * TILE : (t + 1) * TILE] for i in range(run_len)
        ]
        for u, block in enumerate(swap_blocks(blocks, a_width)):
            send[t * group + u] = block.astype(jnp.bfloat16)

    pl.semaphore_wait(barrier, blk_count - 1 + rep_count - 1)

    def send_blk(step, carry):
        ring = step // 2
        far = chips // 2 - (ring + 1) // 2
        shift = jnp.where(ring % 2 == 1, far, chips - far)
        other = lax.rem(me_p // 2 + shift, chips) * 2 + lax.rem(me_p + 1 + step, 2)
        pltpu.make_async_remote_copy(
            src_ref=send.at[other],
            dst_ref=recv.at[me_p],
            send_sem=send_sem,
            recv_sem=recv_sem,
            device_id={"blk": other},
            device_id_type=MESH,
        ).start()
        return carry

    lax.fori_loop(0, blk_count - 1, send_blk, 0)
    recv[me_p] = send[me_p]

    w_copy.wait()
    wanted = k_ref[0] ^ j_ref[0]

    def turn(t, carry):
        rows = pl.ds(pl.multiple_of(t * TILE, TILE), TILE)
        for b in range(tiles):
            tile = w_vm[rows, b * TILE : (b + 1) * TILE].astype(jnp.float32)
            tile = jnp.where(tile_ref[t] ^ irreps[b] == wanted, tile, 0.0)
            wt_vm[b * TILE : (b + 1) * TILE, rows] = tile.T.astype(jnp.bfloat16)
        return carry

    lax.fori_loop(0, tiles, turn, 0)

    others = pl.ds(0, blk_count - 1)
    pltpu.make_async_copy(send.at[others], recv.at[others], recv_sem).wait()
    left = recv[...].reshape(full, TILE)
    part = jnp.dot(wt_vm[...], left, preferred_element_type=jnp.float32)
    part_send[...] = part.reshape(rep_count, b_width, TILE)

    def send_rep(step, carry):
        other = lax.rem(me_r + step, rep_count)
        pltpu.make_async_remote_copy(
            src_ref=part_send.at[other],
            dst_ref=part_recv.at[me_r],
            send_sem=part_send_sem,
            recv_sem=part_recv_sem,
            device_id={"rep": other},
            device_id_type=MESH,
        ).start()
        return carry

    lax.fori_loop(1, rep_count, send_rep, 0)
    part_recv[me_r] = part_send[me_r]
    pltpu.make_async_copy(send.at[others], recv.at[others], send_sem).wait()
    others = pl.ds(0, rep_count - 1)
    pltpu.make_async_copy(part_send.at[others], part_recv.at[others], part_recv_sem).wait()
    total = part_recv[0]
    for r in range(1, rep_count):
        total = total + part_recv[r]
    out_ref[...] = total
    pltpu.make_async_copy(part_send.at[others], part_recv.at[others], part_send_sem).wait()


def shards(t_slab, w_cycle, k_irrep, i_irrep, j_irrep, tile_irrep, i_energy, j_energy, vir_energy):
    blk_count = lax.axis_size("blk")
    rep_count = lax.axis_size("rep")
    _, c_width, rows_i, full = t_slab.shape
    tiles = full // TILE
    run_len = rows_i // RUNS
    a_width = full // blk_count
    b_width = full // rep_count
    packed = run_len * a_width
    smem = pl.BlockSpec(memory_space=pltpu.SMEM)
    hbm = pl.BlockSpec(memory_space=pl.ANY)
    summed = pl.pallas_call(
        functools.partial(kernel, blk_count, rep_count),
        out_shape=jax.ShapeDtypeStruct((b_width, packed), jnp.float32),
        in_specs=[smem, smem, smem, smem, hbm, hbm],
        out_specs=pl.BlockSpec(memory_space=pltpu.VMEM),
        scratch_shapes=[
            pltpu.VMEM((c_width, rows_i, full), jnp.bfloat16),
            pltpu.VMEM((full, full), jnp.bfloat16),
            pltpu.VMEM((run_len * c_width, full), jnp.float32),
            pltpu.VMEM((full, full), jnp.bfloat16),
            pltpu.VMEM((blk_count, c_width, packed), jnp.bfloat16),
            pltpu.VMEM((blk_count, c_width, packed), jnp.bfloat16),
            pltpu.VMEM((rep_count, b_width, packed), jnp.float32),
            pltpu.VMEM((rep_count, b_width, packed), jnp.float32),
            pltpu.SemaphoreType.DMA((2,)),
            pltpu.SemaphoreType.DMA,
            pltpu.SemaphoreType.DMA,
            pltpu.SemaphoreType.DMA,
            pltpu.SemaphoreType.DMA,
        ],
        compiler_params=pltpu.CompilerParams(
            collective_id=0, has_side_effects=True, vmem_limit_bytes=32 * 2**20
        ),
    )(k_irrep, i_irrep, j_irrep, tile_irrep, t_slab[0], w_cycle[0, 0])

    p = lax.axis_index("blk")
    r = lax.axis_index("rep")
    a_energy = lax.dynamic_slice_in_dim(vir_energy, p * a_width, a_width, 0)
    b_energy = lax.dynamic_slice_in_dim(vir_energy, r * b_width, b_width, 0)
    a_irrep = tile_irrep[p * a_width // TILE]
    b_irrep = tile_irrep[r * b_width // TILE]
    value = summed.T.reshape(1, run_len, a_width, b_width)
    keep = i_irrep == (j_irrep[0] ^ a_irrep ^ b_irrep)
    denom = (
        a_energy[None, :, None]
        + b_energy[None, None, :]
        - i_energy[:, None, None]
        - j_energy[:, None, None]
    ).reshape(RUNS, run_len, a_width, b_width)
    keep = keep.reshape(RUNS, run_len, 1, 1)
    result = jnp.where(keep, value / denom, 0.0)
    return result.reshape(1, rows_i, a_width, b_width)


def solution(mesh):
    in_specs = (
        P("rep", "blk", None, None),
        P("rep", None, None, None),
        P("rep"),
        P(),
        P(),
        P(),
        P(),
        P(),
        P(),
    )
    out_specs = P(None, None, "blk", "rep")
    return jax.shard_map(shards, mesh=mesh, in_specs=in_specs, out_specs=out_specs, check_vma=False)
```

```python
import functools

import jax
import jax.numpy as jnp
from jax import lax
from jax.experimental import pallas as pl
from jax.experimental.pallas import tpu as pltpu
from jax.sharding import PartitionSpec as P

TILE = 128
RUNS = 8
FIRST_TILES = 2
AHEAD = 8
HALF = TILE // 2
MESH = pl.DeviceIdType.MESH


def pick(position, scalars):
    label = jnp.zeros(position.shape, jnp.int32)
    for place, scalar in enumerate(scalars):
        label = jnp.where(position == place, scalar, label)
    return label


def swap_blocks(rows, width):
    count = len(rows)
    block = lax.broadcasted_iota(jnp.int32, rows[0].shape, 1) // width
    step = count // 2
    while step:
        low = (block // step) % 2 == 0
        new = list(rows)
        for i in range(count):
            if i & step == 0:
                j = i | step
                new[i] = jnp.where(low, rows[i], pltpu.roll(rows[j], step * width, 1))
                new[j] = jnp.where(low, pltpu.roll(rows[i], TILE - step * width, 1), rows[j])
        rows = new
        step //= 2
    return rows


def kernel(
    blk_count,
    rep_count,
    k_hbm,
    i_hbm,
    j_hbm,
    tile_hbm,
    i_energy_hbm,
    j_energy_hbm,
    vir_hbm,
    t_hbm,
    w_hbm,
    out_ref,
    k_ref,
    i_ref,
    j_ref,
    tile_ref,
    i_energy,
    j_energy,
    vir_vm,
    t_vm,
    w_vm,
    wt_vm,
    denom_vm,
    left_vm,
    send,
    recv,
    part_send,
    part_recv,
    small_sem,
    t_sem,
    w_sem,
    ok_sem,
    here_sem,
    send_sem,
    recv_sem,
    part_send_sem,
    part_recv_sem,
):
    tiles, c_width, rows_i, _ = t_vm.shape
    full = tiles * TILE
    run_len = rows_i // RUNS
    group = blk_count // tiles
    a_width = full // blk_count
    b_width = full // rep_count
    chips = blk_count // 2
    first_tiles = FIRST_TILES
    first = first_tiles * group // 2
    me_p = lax.axis_index("blk")
    me_r = lax.axis_index("rep")
    chip = me_p // 2
    core = lax.rem(me_p, 2)
    sibling = me_p + 1 - 2 * core

    small = [
        pltpu.make_async_copy(source, target, small_sem.at[n])
        for n, (source, target) in enumerate(
            (
                (k_hbm, k_ref),
                (i_hbm, i_ref),
                (tile_hbm, tile_ref),
                (j_hbm, j_ref),
                (i_energy_hbm, i_energy),
                (j_energy_hbm, j_energy),
                (vir_hbm, vir_vm),
            )
        )
    ]
    for copy in small[:3]:
        copy.start()
    t_copies = [
        pltpu.make_async_copy(t_hbm.at[:, :, pl.ds(t * TILE, TILE)], t_vm.at[t], t_sem.at[t])
        for t in range(tiles)
    ]
    for copy in t_copies:
        copy.start()

    barrier = pltpu.get_barrier_semaphore()
    is_first = chip < first
    before = jnp.minimum(chip, first)

    def greet(**device):
        pl.semaphore_signal(barrier, inc=1, device_id=device, device_id_type=MESH)

    def greet_after(other, carry):
        greet(blk=other * 2)
        return carry

    def greet_last(other, carry):
        @pl.when(other != chip)
        def _():
            greet(blk=other * 2 + 1)

        return carry

    def greet_rep(step, carry):
        greet(blk=chip * 2 + 1, rep=lax.rem(me_r + step, rep_count))
        return carry

    greet(blk=sibling)

    @pl.when(is_first)
    def _():
        lax.fori_loop(chip + 1, chips, greet_after, 0)

    @pl.when(jnp.logical_not(is_first))
    def _():
        lax.fori_loop(first, chips, greet_last, 0)

    lax.fori_loop(1, rep_count, greet_rep, 0)

    w_copy = pltpu.make_async_copy(w_hbm, w_vm, w_sem)
    w_copy.start()
    for copy in small[3:]:
        copy.start()

    row = lax.broadcasted_iota(jnp.int32, (run_len * c_width, 16 * c_width), 0)
    col = lax.broadcasted_iota(jnp.int32, (run_len * c_width, 16 * c_width), 1)
    chosen = (row % c_width == col // 16) & (row // c_width == col % run_len)
    order = jnp.where(chosen, 1.0, 0.0).astype(jnp.bfloat16)
    for copy in small[:3]:
        copy.wait()
    irreps = [tile_ref[t] for t in range(tiles)]
    row = lax.broadcasted_iota(jnp.int32, (rows_i, TILE), 0)
    run_label = pick(row // run_len, [i_ref[g * run_len] for g in range(RUNS)])
    run_label = run_label ^ (k_ref[0] ^ tile_ref[me_p // group])

    low = lax.broadcasted_iota(jnp.int32, (8, TILE), 1) < HALF

    def pack(t, carry):
        lanes = pl.ds(pl.multiple_of(t * TILE, TILE), TILE)
        pltpu.make_async_copy(t_hbm.at[:, :, lanes], t_vm.at[t], t_sem.at[t]).wait()
        mask = jnp.where(run_label == tile_ref[t], 1.0, 0.0).astype(jnp.bfloat16)
        held = t_vm[t] * mask[None]
        held = sum(held[:, 16 * q : 16 * q + 16] for q in range(rows_i // 16))
        held = held.reshape(c_width * 16, TILE)
        held = jnp.dot(order, held, preferred_element_type=jnp.float32)
        blocks = [held[i * c_width : (i + 1) * c_width] for i in range(run_len)]
        for u, block in enumerate(swap_blocks(blocks, a_width)):
            above, below = block[:8], block[8:]
            one = jnp.where(low, above, pltpu.roll(below, HALF, 1))
            two = jnp.where(low, pltpu.roll(above, HALF, 1), below)
            send[0, t * group + u] = one.astype(jnp.bfloat16)
            send[1, t * group + u] = two.astype(jnp.bfloat16)
        return carry

    def send_to(half, other):
        pltpu.make_async_remote_copy(
            src_ref=send.at[half, other],
            dst_ref=recv.at[half, me_p],
            send_sem=send_sem.at[half],
            recv_sem=recv_sem.at[half],
            device_id={"blk": other},
            device_id_type=MESH,
        ).start()

    @pl.when(core == 0)
    def _():
        pl.semaphore_wait(barrier, 2 * before + 1)
        pl.semaphore_signal(ok_sem, inc=1, device_id={"blk": sibling}, device_id_type=MESH)

    @pl.when(core == 1)
    def _():
        pl.semaphore_wait(ok_sem, 1)

    def tell(other, carry):
        pl.semaphore_signal(
            here_sem.at[chip], inc=1, device_id={"blk": other * 2 + core}, device_id_type=MESH
        )
        return carry

    lax.fori_loop(0, before, tell, 0)
    lax.fori_loop(0, first_tiles, pack, 0)

    ahead = 2 * jnp.where(is_first, first, AHEAD)

    def send_before(step, carry):
        other = lax.rem(step, ahead)

        @pl.when((other // 2 < chip) | (other == sibling))
        def _():
            send_to(step // ahead, other)

        return carry

    lax.fori_loop(0, 2 * ahead, send_before, 0)

    lax.fori_loop(first_tiles, tiles, pack, 0)

    def send_chip(half, other):
        @pl.when(half == 0)
        def _():
            pl.semaphore_wait(here_sem.at[other], 1)

        send_to(half, other * 2 + core)
        send_to(half, other * 2 + 1 - core)

    def send_after(other, half):
        send_chip(half, other)
        return half

    def send_later(step, half):
        turn = step // 3
        place = lax.rem(step, 3)
        send_chip(half, jnp.where(place == 0, first + turn, chips - 2 * turn - place))
        return half

    @pl.when(is_first)
    def _():
        def send_half(half, carry):
            lax.fori_loop(chip + 1, first, send_after, half)
            lax.fori_loop(0, chips - first, send_later, half)
            return carry

        lax.fori_loop(0, 2, send_half, 0)

    @pl.when(core == 1)
    def _():
        greeted = 1 + 2 * (rep_count - 1)
        pl.semaphore_wait(
            barrier, jnp.where(is_first, greeted, greeted + 2 * (chips - first - 1))
        )
        pl.semaphore_signal(ok_sem, inc=1, device_id={"blk": sibling}, device_id_type=MESH)

    @pl.when(core == 0)
    def _():
        pl.semaphore_wait(ok_sem, 1)

    def send_last(step, half):
        ring = step // 2
        far = chips // 2 - (ring + 1) // 2
        shift = jnp.where(ring % 2 == 1, far, chips - far)
        other = lax.rem(chip + shift, chips) * 2 + lax.rem(me_p + 1 + step, 2)

        @pl.when(other >= 2 * AHEAD)
        def _():
            send_to(half, other)

        return half

    @pl.when(jnp.logical_not(is_first))
    def _():
        def send_half(half, carry):
            lax.fori_loop(0, blk_count - 1, send_last, half)
            return carry

        lax.fori_loop(0, 2, send_half, 0)

    for half in range(2):
        recv[half, me_p] = send[half, me_p]

    for copy in small[3:]:
        copy.wait()
    wanted = k_ref[0] ^ j_ref[0]
    w_copy.wait()

    def turn(t, carry):
        rows = pl.ds(pl.multiple_of(t * TILE, TILE), TILE)
        for b in range(tiles):
            tile = w_vm[rows, b * TILE : (b + 1) * TILE].astype(jnp.float32)
            tile = jnp.where(tile_ref[t] ^ irreps[b] == wanted, tile, 0.0)
            tile = tile.reshape(group, 2, 8, TILE)
            tile = jnp.concatenate([tile[:, n].reshape(HALF, TILE) for n in range(2)], axis=0)
            wt_vm[b * TILE : (b + 1) * TILE, rows] = tile.T.astype(jnp.bfloat16)
        return carry

    lax.fori_loop(0, tiles, turn, 0)

    a_start = me_p * a_width
    b_start = me_r * b_width
    run_wanted = j_ref[0] ^ tile_ref[a_start // TILE] ^ tile_ref[b_start // TILE]
    met = [i_ref[g * run_len] == run_wanted for g in range(RUNS)]
    row = lax.broadcasted_iota(jnp.int32, (a_width, TILE), 0)
    col = lax.broadcasted_iota(jnp.int32, (a_width, TILE), 1)
    a_row = vir_vm[pl.ds(a_start // TILE, 1), :]
    a_energy = jnp.sum(
        jnp.where(col == row + lax.rem(a_start, TILE), a_row, 0.0), axis=1, keepdims=True
    )
    b_row = vir_vm[pl.ds(b_start // TILE, 1), :]
    b_row = jnp.where(lax.rem(b_start, TILE) == 0, b_row, pltpu.roll(b_row, TILE - b_width, 1))
    for i in range(run_len):
        energy = i_energy[i]
        for g in range(1, RUNS):
            energy = jnp.where(met[g], i_energy[g * run_len + i], energy)
        rows = pl.ds(i * a_width, a_width)
        denom_vm[rows] = a_energy + b_row - energy - j_energy[0]

    others = pl.ds(0, blk_count - 1)
    wide_low = lax.broadcasted_iota(jnp.int32, (b_width // 2, TILE), 1) < HALF
    side = 4
    lines = side * b_width

    def send_rep(step, half):
        other = (lax.rem(me_r // side + step // side, side)) * side + lax.rem(me_r + step, side)

        @pl.when(other != me_r)
        def _():
            pltpu.make_async_remote_copy(
                src_ref=part_send.at[half, other],
                dst_ref=part_recv.at[half, me_r],
                send_sem=part_send_sem.at[half],
                recv_sem=part_recv_sem.at[half],
                device_id={"rep": other},
                device_id_type=MESH,
            ).start()

        return half

    for half in range(2):
        pltpu.make_async_copy(
            send.at[half, others], recv.at[half, others], recv_sem.at[half]
        ).wait()
        pieces = []
        for t in range(tiles):
            piece = recv[half, t * group : (t + 1) * group].astype(jnp.float32)
            piece = piece.reshape(HALF, TILE)
            pieces += [piece, pltpu.roll(piece, HALF, 1)]
        left_vm[...] = jnp.concatenate(pieces, axis=0).astype(jnp.bfloat16)

        def reduce(step, carry, half=half):
            block = lax.rem(me_r // side + step, side)
            rows = pl.ds(pl.multiple_of(block * lines, lines), lines)
            part = jnp.dot(wt_vm[rows, :], left_vm[...], preferred_element_type=jnp.float32)
            for n in range(side):
                above = part[n * b_width : n * b_width + b_width // 2]
                below = part[n * b_width + b_width // 2 : (n + 1) * b_width]
                part_send[half, block * side + n] = jnp.where(
                    wide_low, above, pltpu.roll(below, HALF, 1)
                )
            lax.fori_loop(step * side, (step + 1) * side, send_rep, half)
            return carry

        lax.fori_loop(0, side, reduce, 0)
        part_recv[half, me_r] = part_send[half, me_r]
    peers = pl.ds(0, rep_count - 1)
    totals = []
    for half in range(2):
        pltpu.make_async_copy(
            part_send.at[half, peers], part_recv.at[half, peers], part_recv_sem.at[half]
        ).wait()
        total = part_recv[half, 0]
        for r in range(1, rep_count):
            total = total + part_recv[half, r]
        totals.append(total)
    above = jnp.where(wide_low, totals[0], pltpu.roll(totals[1], HALF, 1))
    below = jnp.where(wide_low, pltpu.roll(totals[0], HALF, 1), totals[1])
    value = jnp.concatenate([above, below], axis=0).T / denom_vm[:, :b_width]
    for i in range(run_len):
        block = value[i * a_width : (i + 1) * a_width]
        for g in range(RUNS):
            out_ref[g * run_len + i] = jnp.where(met[g], block, 0.0)
    for half in range(2):
        pltpu.make_async_copy(
            send.at[half, others], recv.at[half, others], send_sem.at[half]
        ).wait()
        pltpu.make_async_copy(
            part_send.at[half, peers], part_recv.at[half, peers], part_send_sem.at[half]
        ).wait()


def shards(t_slab, w_cycle, k_irrep, i_irrep, j_irrep, tile_irrep, i_energy, j_energy, vir_energy):
    blk_count = lax.axis_size("blk")
    rep_count = lax.axis_size("rep")
    _, c_width, rows_i, full = t_slab.shape
    tiles = full // TILE
    run_len = rows_i // RUNS
    a_width = full // blk_count
    b_width = full // rep_count
    packed = run_len * a_width
    hbm = pl.BlockSpec(memory_space=pltpu.HBM)
    result = pl.pallas_call(
        functools.partial(kernel, blk_count, rep_count),
        out_shape=jax.ShapeDtypeStruct((rows_i, a_width, b_width), jnp.float32),
        in_specs=[hbm] * 9,
        out_specs=pl.BlockSpec(memory_space=pltpu.VMEM),
        scratch_shapes=[
            pltpu.SMEM((1,), jnp.int32),
            pltpu.SMEM((rows_i,), jnp.int32),
            pltpu.SMEM((1,), jnp.int32),
            pltpu.SMEM((tiles,), jnp.int32),
            pltpu.SMEM((rows_i,), jnp.float32),
            pltpu.SMEM((1,), jnp.float32),
            pltpu.VMEM((tiles, TILE), jnp.float32),
            pltpu.VMEM((tiles, c_width, rows_i, TILE), jnp.bfloat16),
            pltpu.VMEM((full, full), jnp.bfloat16),
            pltpu.VMEM((full, full), jnp.bfloat16),
            pltpu.VMEM((packed, TILE), jnp.float32),
            pltpu.VMEM((full, packed), jnp.bfloat16),
            pltpu.VMEM((2, blk_count, c_width // 2, packed), jnp.bfloat16),
            pltpu.VMEM((2, blk_count, c_width // 2, packed), jnp.bfloat16),
            pltpu.VMEM((2, rep_count, b_width // 2, packed), jnp.float32),
            pltpu.VMEM((2, rep_count, b_width // 2, packed), jnp.float32),
            pltpu.SemaphoreType.DMA((7,)),
            pltpu.SemaphoreType.DMA((tiles,)),
            pltpu.SemaphoreType.DMA,
            pltpu.SemaphoreType.REGULAR,
            pltpu.SemaphoreType.REGULAR((blk_count // 2,)),
            pltpu.SemaphoreType.DMA((2,)),
            pltpu.SemaphoreType.DMA((2,)),
            pltpu.SemaphoreType.DMA((2,)),
            pltpu.SemaphoreType.DMA((2,)),
        ],
        compiler_params=pltpu.CompilerParams(
            collective_id=0, has_side_effects=True, vmem_limit_bytes=62 * 2**20
        ),
    )(
        k_irrep,
        i_irrep,
        j_irrep,
        tile_irrep,
        i_energy,
        j_energy,
        vir_energy.reshape(tiles, TILE),
        t_slab[0],
        w_cycle[0, 0],
    )
    return result[None]


def solution(mesh):
    in_specs = (
        P("rep", "blk", None, None),
        P("rep", None, None, None),
        P("rep"),
        P(),
        P(),
        P(),
        P(),
        P(),
        P(),
    )
    out_specs = P(None, None, "blk", "rep")
    return jax.shard_map(shards, mesh=mesh, in_specs=in_specs, out_specs=out_specs, check_vma=False)
```

```python
import functools

import jax
import jax.numpy as jnp
from jax import lax
from jax.experimental import pallas as pl
from jax.experimental.pallas import tpu as pltpu
from jax.sharding import PartitionSpec as P

TILE = 128
RUNS = 8
FIRST_TILES = 2
AHEAD = 8
HALF = TILE // 2
EVERY = 4
MESH = pl.DeviceIdType.MESH


def pick(position, scalars):
    label = jnp.zeros(position.shape, jnp.int32)
    for place, scalar in enumerate(scalars):
        label = jnp.where(position == place, scalar, label)
    return label


def swap_blocks(rows, width):
    count = len(rows)
    block = lax.broadcasted_iota(jnp.int32, rows[0].shape, 1) // width
    step = count // 2
    while step:
        low = (block // step) % 2 == 0
        new = list(rows)
        for i in range(count):
            if i & step == 0:
                j = i | step
                new[i] = jnp.where(low, rows[i], pltpu.roll(rows[j], step * width, 1))
                new[j] = jnp.where(low, pltpu.roll(rows[i], TILE - step * width, 1), rows[j])
        rows = new
        step //= 2
    return rows


def kernel(
    blk_count,
    rep_count,
    k_hbm,
    i_hbm,
    j_hbm,
    tile_hbm,
    i_energy_hbm,
    j_energy_hbm,
    vir_hbm,
    t_hbm,
    w_hbm,
    out_ref,
    k_ref,
    i_ref,
    j_ref,
    tile_ref,
    i_energy,
    j_energy,
    vir_vm,
    t_vm,
    w_vm,
    wt_vm,
    denom_vm,
    left_vm,
    send,
    recv,
    part_send,
    part_recv,
    small_sem,
    t_sem,
    w_sem,
    ok_sem,
    here_sem,
    send_sem,
    recv_sem,
    part_send_sem,
    part_recv_sem,
):
    tiles, c_width, rows_i, _ = t_vm.shape
    full = tiles * TILE
    run_len = rows_i // RUNS
    group = blk_count // tiles
    a_width = full // blk_count
    b_width = full // rep_count
    chips = blk_count // 2
    first_tiles = FIRST_TILES
    first = first_tiles * group // 2
    me_p = lax.axis_index("blk")
    me_r = lax.axis_index("rep")
    chip = me_p // 2
    core = lax.rem(me_p, 2)
    sibling = me_p + 1 - 2 * core

    small = [
        pltpu.make_async_copy(source, target, small_sem.at[n])
        for n, (source, target) in enumerate(
            (
                (k_hbm, k_ref),
                (i_hbm, i_ref),
                (tile_hbm, tile_ref),
                (j_hbm, j_ref),
                (i_energy_hbm, i_energy),
                (j_energy_hbm, j_energy),
                (vir_hbm, vir_vm),
            )
        )
    ]
    for copy in small[:3]:
        copy.start()
    t_copies = [
        pltpu.make_async_copy(t_hbm.at[:, :, pl.ds(t * TILE, TILE)], t_vm.at[t], t_sem.at[t])
        for t in range(tiles)
    ]
    for copy in t_copies:
        copy.start()

    barrier = pltpu.get_barrier_semaphore()
    is_first = chip < first
    before = jnp.minimum(chip, first)

    def greet(**device):
        pl.semaphore_signal(barrier, inc=1, device_id=device, device_id_type=MESH)

    def greet_after(other, carry):
        greet(blk=other * 2)
        return carry

    def greet_last(other, carry):
        @pl.when(other != chip)
        def _():
            greet(blk=other * 2 + 1)

        return carry

    def greet_rep(step, carry):
        greet(blk=chip * 2 + 1, rep=lax.rem(me_r + step, rep_count))
        return carry

    greet(blk=sibling)

    @pl.when(is_first)
    def _():
        lax.fori_loop(chip + 1, chips, greet_after, 0)

    @pl.when(jnp.logical_not(is_first))
    def _():
        lax.fori_loop(first, chips, greet_last, 0)

    lax.fori_loop(1, rep_count, greet_rep, 0)

    w_copy = pltpu.make_async_copy(w_hbm, w_vm, w_sem)
    w_copy.start()
    for copy in small[3:]:
        copy.start()

    row = lax.broadcasted_iota(jnp.int32, (run_len * c_width, 16 * c_width), 0)
    col = lax.broadcasted_iota(jnp.int32, (run_len * c_width, 16 * c_width), 1)
    chosen = (row % c_width == col // 16) & (row // c_width == col % run_len)
    order = jnp.where(chosen, 1.0, 0.0).astype(jnp.bfloat16)
    for copy in small[:3]:
        copy.wait()
    irreps = [tile_ref[t] for t in range(tiles)]
    row = lax.broadcasted_iota(jnp.int32, (rows_i, TILE), 0)
    run_label = pick(row // run_len, [i_ref[g * run_len] for g in range(RUNS)])
    run_label = run_label ^ (k_ref[0] ^ tile_ref[me_p // group])

    low = lax.broadcasted_iota(jnp.int32, (8, TILE), 1) < HALF

    def pack(t, carry):
        lanes = pl.ds(pl.multiple_of(t * TILE, TILE), TILE)
        pltpu.make_async_copy(t_hbm.at[:, :, lanes], t_vm.at[t], t_sem.at[t]).wait()
        mask = jnp.where(run_label == tile_ref[t], 1.0, 0.0).astype(jnp.bfloat16)
        held = t_vm[t] * mask[None]
        held = sum(held[:, 16 * q : 16 * q + 16] for q in range(rows_i // 16))
        held = held.reshape(c_width * 16, TILE)
        held = jnp.dot(order, held, preferred_element_type=jnp.float32)
        blocks = [held[i * c_width : (i + 1) * c_width] for i in range(run_len)]
        for u, block in enumerate(swap_blocks(blocks, a_width)):
            above, below = block[:8], block[8:]
            one = jnp.where(low, above, pltpu.roll(below, HALF, 1))
            two = jnp.where(low, pltpu.roll(above, HALF, 1), below)
            send[0, t * group + u] = one.astype(jnp.bfloat16)
            send[1, t * group + u] = two.astype(jnp.bfloat16)
        return carry

    def send_to(half, other):
        pltpu.make_async_remote_copy(
            src_ref=send.at[half, other],
            dst_ref=recv.at[half, me_p],
            send_sem=send_sem.at[half],
            recv_sem=recv_sem.at[half],
            device_id={"blk": other},
            device_id_type=MESH,
        ).start()

    @pl.when(core == 0)
    def _():
        pl.semaphore_wait(barrier, 2 * before + 1)
        pl.semaphore_signal(ok_sem, inc=1, device_id={"blk": sibling}, device_id_type=MESH)

    @pl.when(core == 1)
    def _():
        pl.semaphore_wait(ok_sem, 1)

    def tell(other, carry):
        pl.semaphore_signal(
            here_sem.at[chip], inc=1, device_id={"blk": other * 2 + core}, device_id_type=MESH
        )
        return carry

    lax.fori_loop(0, before, tell, 0)
    lax.fori_loop(0, first_tiles, pack, 0)

    ahead = 2 * jnp.where(is_first, first, AHEAD)

    def send_before(step, carry):
        other = lax.rem(step, ahead)

        @pl.when((other // 2 < chip) | (other == sibling))
        def _():
            send_to(step // ahead, other)

        return carry

    in_time = chip < chips // 2
    lax.fori_loop(0, jnp.where(in_time, 2, 1) * ahead, send_before, 0)

    lax.fori_loop(first_tiles, tiles, pack, 0)

    for copy in small[3:]:
        copy.wait()
    wanted = k_ref[0] ^ j_ref[0]
    w_copy.wait()

    def turn(t, carry):
        rows = pl.ds(pl.multiple_of(t * TILE, TILE), TILE)
        for b in range(tiles):
            tile = w_vm[rows, b * TILE : (b + 1) * TILE].astype(jnp.float32)
            tile = jnp.where(tile_ref[t] ^ irreps[b] == wanted, tile, 0.0)
            tile = tile.reshape(group, 2, 8, TILE)
            tile = jnp.concatenate([tile[:, n].reshape(HALF, TILE) for n in range(2)], axis=0)
            wt_vm[b * TILE : (b + 1) * TILE, rows] = tile.T.astype(jnp.bfloat16)
        return carry

    lax.fori_loop(0, tiles, turn, 0)

    a_start = me_p * a_width
    b_start = me_r * b_width
    run_wanted = j_ref[0] ^ tile_ref[a_start // TILE] ^ tile_ref[b_start // TILE]
    met = [i_ref[g * run_len] == run_wanted for g in range(RUNS)]
    row = lax.broadcasted_iota(jnp.int32, (a_width, TILE), 0)
    col = lax.broadcasted_iota(jnp.int32, (a_width, TILE), 1)
    a_row = vir_vm[pl.ds(a_start // TILE, 1), :]
    a_energy = jnp.sum(
        jnp.where(col == row + lax.rem(a_start, TILE), a_row, 0.0), axis=1, keepdims=True
    )
    b_row = vir_vm[pl.ds(b_start // TILE, 1), :]
    b_row = jnp.where(lax.rem(b_start, TILE) == 0, b_row, pltpu.roll(b_row, TILE - b_width, 1))
    for i in range(run_len):
        energy = i_energy[i]
        for g in range(1, RUNS):
            energy = jnp.where(met[g], i_energy[g * run_len + i], energy)
        rows = pl.ds(i * a_width, a_width)
        denom_vm[rows] = a_energy + b_row - energy - j_energy[0]

    def send_chip(half, other):
        @pl.when(half == 0)
        def _():
            pl.semaphore_wait(here_sem.at[other], 1)

        send_to(half, other * 2 + core)
        send_to(half, other * 2 + 1 - core)

    def send_after(other, half):
        send_chip(half, other)
        return half

    def send_later(step, half):
        turn = step // 3
        place = lax.rem(step, 3)
        send_chip(half, jnp.where(place == 0, first + turn, chips - 2 * turn - place))
        return half

    @pl.when(is_first)
    def _():
        def send_half(half, carry):
            lax.fori_loop(chip + 1, first, send_after, half)
            lax.fori_loop(0, chips - first, send_later, half)
            return carry

        lax.fori_loop(0, 2, send_half, 0)

    @pl.when(core == 1)
    def _():
        greeted = 1 + 2 * (rep_count - 1)
        pl.semaphore_wait(
            barrier, jnp.where(is_first, greeted, greeted + 2 * (chips - first - 1))
        )
        pl.semaphore_signal(ok_sem, inc=1, device_id={"blk": sibling}, device_id_type=MESH)

    @pl.when(core == 0)
    def _():
        pl.semaphore_wait(ok_sem, 1)

    def send_last(step, half):
        place = jnp.where(lax.rem(step, 2) == 0, step // 2, blk_count - 2 - step // 2)
        ring = place // 2
        far = chips // 2 - (ring + 1) // 2
        shift = jnp.where(ring % 2 == 1, far, chips - far)
        other = lax.rem(chip + shift, chips) * 2 + lax.rem(me_p + 1 + place, 2)

        @pl.when((other >= 2 * AHEAD) & (step < blk_count - 1))
        def _():
            send_to(half, other)

        turn = step // EVERY

        @pl.when((half == 0) & (lax.rem(step, EVERY) == EVERY - 1) & (turn < 2 * AHEAD) & jnp.logical_not(in_time))
        def _():
            send_to(1, turn)

        return half

    @pl.when(jnp.logical_not(is_first))
    def _():
        def send_half(half, carry):
            lax.fori_loop(0, blk_count, send_last, half)
            return carry

        lax.fori_loop(0, 2, send_half, 0)

    for half in range(2):
        recv[half, me_p] = send[half, me_p]

    others = pl.ds(0, blk_count - 1)
    wide_low = lax.broadcasted_iota(jnp.int32, (b_width // 2, TILE), 1) < HALF
    side = 4
    lines = side * b_width

    def send_rep(step, half):
        other = (lax.rem(me_r // side + step // side, side)) * side + lax.rem(me_r + step, side)

        @pl.when(other != me_r)
        def _():
            pltpu.make_async_remote_copy(
                src_ref=part_send.at[half, other],
                dst_ref=part_recv.at[half, me_r],
                send_sem=part_send_sem.at[half],
                recv_sem=part_recv_sem.at[half],
                device_id={"rep": other},
                device_id_type=MESH,
            ).start()

        return half

    for half in range(2):
        pltpu.make_async_copy(
            send.at[half, others], recv.at[half, others], recv_sem.at[half]
        ).wait()
        pieces = []
        for t in range(tiles):
            piece = recv[half, t * group : (t + 1) * group].astype(jnp.float32)
            piece = piece.reshape(HALF, TILE)
            pieces += [piece, pltpu.roll(piece, HALF, 1)]
        left_vm[...] = jnp.concatenate(pieces, axis=0).astype(jnp.bfloat16)

        def reduce(step, carry, half=half):
            block = lax.rem(me_r // side + step, side)
            rows = pl.ds(pl.multiple_of(block * lines, lines), lines)
            part = jnp.dot(wt_vm[rows, :], left_vm[...], preferred_element_type=jnp.float32)
            for n in range(side):
                above = part[n * b_width : n * b_width + b_width // 2]
                below = part[n * b_width + b_width // 2 : (n + 1) * b_width]
                part_send[half, block * side + n] = jnp.where(
                    wide_low, above, pltpu.roll(below, HALF, 1)
                )
            lax.fori_loop(step * side, (step + 1) * side, send_rep, half)
            return carry

        lax.fori_loop(0, side, reduce, 0)
        part_recv[half, me_r] = part_send[half, me_r]
    peers = pl.ds(0, rep_count - 1)
    totals = []
    for half in range(2):
        pltpu.make_async_copy(
            part_send.at[half, peers], part_recv.at[half, peers], part_recv_sem.at[half]
        ).wait()
        total = part_recv[half, 0]
        for r in range(1, rep_count):
            total = total + part_recv[half, r]
        totals.append(total)
    above = jnp.where(wide_low, totals[0], pltpu.roll(totals[1], HALF, 1))
    below = jnp.where(wide_low, pltpu.roll(totals[0], HALF, 1), totals[1])
    value = jnp.concatenate([above, below], axis=0).T / denom_vm[:, :b_width]
    for i in range(run_len):
        block = value[i * a_width : (i + 1) * a_width]
        for g in range(RUNS):
            out_ref[g * run_len + i] = jnp.where(met[g], block, 0.0)
    for half in range(2):
        pltpu.make_async_copy(
            send.at[half, others], recv.at[half, others], send_sem.at[half]
        ).wait()
        pltpu.make_async_copy(
            part_send.at[half, peers], part_recv.at[half, peers], part_send_sem.at[half]
        ).wait()


def shards(t_slab, w_cycle, k_irrep, i_irrep, j_irrep, tile_irrep, i_energy, j_energy, vir_energy):
    blk_count = lax.axis_size("blk")
    rep_count = lax.axis_size("rep")
    _, c_width, rows_i, full = t_slab.shape
    tiles = full // TILE
    run_len = rows_i // RUNS
    a_width = full // blk_count
    b_width = full // rep_count
    packed = run_len * a_width
    hbm = pl.BlockSpec(memory_space=pltpu.HBM)
    held = functools.partial(pltpu.with_memory_space_constraint, memory_space=pltpu.HBM)
    result = pl.pallas_call(
        functools.partial(kernel, blk_count, rep_count),
        out_shape=jax.ShapeDtypeStruct((rows_i, a_width, b_width), jnp.float32),
        in_specs=[hbm] * 9,
        out_specs=pl.BlockSpec(memory_space=pltpu.VMEM),
        scratch_shapes=[
            pltpu.SMEM((1,), jnp.int32),
            pltpu.SMEM((rows_i,), jnp.int32),
            pltpu.SMEM((1,), jnp.int32),
            pltpu.SMEM((tiles,), jnp.int32),
            pltpu.SMEM((rows_i,), jnp.float32),
            pltpu.SMEM((1,), jnp.float32),
            pltpu.VMEM((tiles, TILE), jnp.float32),
            pltpu.VMEM((tiles, c_width, rows_i, TILE), jnp.bfloat16),
            pltpu.VMEM((full, full), jnp.bfloat16),
            pltpu.VMEM((full, full), jnp.bfloat16),
            pltpu.VMEM((packed, TILE), jnp.float32),
            pltpu.VMEM((full, packed), jnp.bfloat16),
            pltpu.VMEM((2, blk_count, c_width // 2, packed), jnp.bfloat16),
            pltpu.VMEM((2, blk_count, c_width // 2, packed), jnp.bfloat16),
            pltpu.VMEM((2, rep_count, b_width // 2, packed), jnp.float32),
            pltpu.VMEM((2, rep_count, b_width // 2, packed), jnp.float32),
            pltpu.SemaphoreType.DMA((7,)),
            pltpu.SemaphoreType.DMA((tiles,)),
            pltpu.SemaphoreType.DMA,
            pltpu.SemaphoreType.REGULAR,
            pltpu.SemaphoreType.REGULAR((blk_count // 2,)),
            pltpu.SemaphoreType.DMA((2,)),
            pltpu.SemaphoreType.DMA((2,)),
            pltpu.SemaphoreType.DMA((2,)),
            pltpu.SemaphoreType.DMA((2,)),
        ],
        compiler_params=pltpu.CompilerParams(
            collective_id=0, has_side_effects=True, vmem_limit_bytes=40 * 2**20
        ),
    )(
        k_irrep,
        held(i_irrep),
        j_irrep,
        held(tile_irrep),
        held(i_energy),
        j_energy,
        held(vir_energy.reshape(tiles, TILE)),
        held(t_slab[0]),
        held(w_cycle[0, 0]),
    )
    return result[None]


def solution(mesh):
    in_specs = (
        P("rep", "blk", None, None),
        P("rep", None, None, None),
        P("rep"),
        P(),
        P(),
        P(),
        P(),
        P(),
        P(),
    )
    out_specs = P(None, None, "blk", "rep")
    return jax.shard_map(shards, mesh=mesh, in_specs=in_specs, out_specs=out_specs, check_vma=False)
```

```python
import functools

import jax
import jax.numpy as jnp
from jax import lax
from jax.experimental import pallas as pl
from jax.experimental.pallas import tpu as pltpu
from jax.sharding import PartitionSpec as P

TILE = 128
RUNS = 8
FIRST_TILES = 2
AHEAD = 8
HALF = TILE // 2
EVERY = 1
MESH = pl.DeviceIdType.MESH


def pick(position, scalars):
    label = jnp.zeros(position.shape, jnp.int32)
    for place, scalar in enumerate(scalars):
        label = jnp.where(position == place, scalar, label)
    return label


def swap_blocks(rows, width):
    count = len(rows)
    block = lax.broadcasted_iota(jnp.int32, rows[0].shape, 1) // width
    step = count // 2
    while step:
        low = (block // step) % 2 == 0
        new = list(rows)
        for i in range(count):
            if i & step == 0:
                j = i | step
                new[i] = jnp.where(low, rows[i], pltpu.roll(rows[j], step * width, 1))
                new[j] = jnp.where(low, pltpu.roll(rows[i], TILE - step * width, 1), rows[j])
        rows = new
        step //= 2
    return rows


def kernel(
    blk_count,
    rep_count,
    k_hbm,
    i_hbm,
    j_hbm,
    tile_hbm,
    i_energy_hbm,
    j_energy_hbm,
    vir_hbm,
    t_hbm,
    w_hbm,
    out_ref,
    k_ref,
    i_ref,
    j_ref,
    tile_ref,
    i_energy,
    j_energy,
    vir_vm,
    t_vm,
    w_vm,
    wt_vm,
    denom_vm,
    left_vm,
    send,
    recv,
    part_send,
    part_recv,
    small_sem,
    t_sem,
    w_sem,
    ok_sem,
    here_sem,
    send_sem,
    recv_sem,
    part_send_sem,
    part_recv_sem,
):
    tiles, c_width, rows_i, _ = t_vm.shape
    full = tiles * TILE
    run_len = rows_i // RUNS
    group = blk_count // tiles
    a_width = full // blk_count
    b_width = full // rep_count
    chips = blk_count // 2
    first_tiles = FIRST_TILES
    first = first_tiles * group // 2
    me_p = lax.axis_index("blk")
    me_r = lax.axis_index("rep")
    chip = me_p // 2
    core = lax.rem(me_p, 2)
    sibling = me_p + 1 - 2 * core

    small = [
        pltpu.make_async_copy(source, target, small_sem.at[n])
        for n, (source, target) in enumerate(
            (
                (k_hbm, k_ref),
                (i_hbm, i_ref),
                (tile_hbm, tile_ref),
                (j_hbm, j_ref),
                (i_energy_hbm, i_energy),
                (j_energy_hbm, j_energy),
                (vir_hbm, vir_vm),
            )
        )
    ]
    for copy in small[:3]:
        copy.start()
    t_copies = [
        pltpu.make_async_copy(t_hbm.at[:, :, pl.ds(t * TILE, TILE)], t_vm.at[t], t_sem.at[t])
        for t in range(tiles)
    ]
    for copy in t_copies:
        copy.start()

    barrier = pltpu.get_barrier_semaphore()
    is_first = chip < first
    before = jnp.minimum(chip, first)

    def greet(**device):
        pl.semaphore_signal(barrier, inc=1, device_id=device, device_id_type=MESH)

    def greet_after(other, carry):
        greet(blk=other * 2)
        return carry

    def greet_last(other, carry):
        @pl.when(other != chip)
        def _():
            greet(blk=other * 2 + 1)

        return carry

    def greet_rep(step, carry):
        greet(blk=chip * 2 + 1, rep=lax.rem(me_r + step, rep_count))
        return carry

    greet(blk=sibling)

    @pl.when(is_first)
    def _():
        lax.fori_loop(chip + 1, chips, greet_after, 0)

    @pl.when(jnp.logical_not(is_first))
    def _():
        lax.fori_loop(first, chips, greet_last, 0)

    lax.fori_loop(1, rep_count, greet_rep, 0)

    w_copy = pltpu.make_async_copy(w_hbm, w_vm, w_sem)
    w_copy.start()
    for copy in small[3:]:
        copy.start()

    row = lax.broadcasted_iota(jnp.int32, (run_len * c_width, 16 * c_width), 0)
    col = lax.broadcasted_iota(jnp.int32, (run_len * c_width, 16 * c_width), 1)
    chosen = (row % c_width == col // 16) & (row // c_width == col % run_len)
    order = jnp.where(chosen, 1.0, 0.0).astype(jnp.bfloat16)
    for copy in small[:3]:
        copy.wait()
    irreps = [tile_ref[t] for t in range(tiles)]
    row = lax.broadcasted_iota(jnp.int32, (rows_i, TILE), 0)
    run_label = pick(row // run_len, [i_ref[g * run_len] for g in range(RUNS)])
    run_label = run_label ^ (k_ref[0] ^ tile_ref[me_p // group])

    low = lax.broadcasted_iota(jnp.int32, (8, TILE), 1) < HALF

    def pack(t, carry):
        lanes = pl.ds(pl.multiple_of(t * TILE, TILE), TILE)
        pltpu.make_async_copy(t_hbm.at[:, :, lanes], t_vm.at[t], t_sem.at[t]).wait()
        mask = jnp.where(run_label == tile_ref[t], 1.0, 0.0).astype(jnp.bfloat16)
        held = t_vm[t] * mask[None]
        held = sum(held[:, 16 * q : 16 * q + 16] for q in range(rows_i // 16))
        held = held.reshape(c_width * 16, TILE)
        held = jnp.dot(order, held, preferred_element_type=jnp.float32)
        blocks = [held[i * c_width : (i + 1) * c_width] for i in range(run_len)]
        for u, block in enumerate(swap_blocks(blocks, a_width)):
            above, below = block[:8], block[8:]
            one = jnp.where(low, above, pltpu.roll(below, HALF, 1))
            two = jnp.where(low, pltpu.roll(above, HALF, 1), below)
            send[0, t * group + u] = one.astype(jnp.bfloat16)
            send[1, t * group + u] = two.astype(jnp.bfloat16)
        return carry

    def send_to(half, other):
        pltpu.make_async_remote_copy(
            src_ref=send.at[half, other],
            dst_ref=recv.at[half, me_p],
            send_sem=send_sem.at[half],
            recv_sem=recv_sem.at[half],
            device_id={"blk": other},
            device_id_type=MESH,
        ).start()

    @pl.when(core == 0)
    def _():
        pl.semaphore_wait(barrier, 2 * before + 1)
        pl.semaphore_signal(ok_sem, inc=1, device_id={"blk": sibling}, device_id_type=MESH)

    @pl.when(core == 1)
    def _():
        pl.semaphore_wait(ok_sem, 1)

    def tell(other, carry):
        pl.semaphore_signal(
            here_sem.at[chip], inc=1, device_id={"blk": other * 2 + core}, device_id_type=MESH
        )
        return carry

    lax.fori_loop(0, before, tell, 0)
    lax.fori_loop(0, first_tiles, pack, 0)

    ahead = 2 * jnp.where(is_first, first, AHEAD)

    def send_before(step, carry):
        other = lax.rem(step, ahead)

        @pl.when((other // 2 < chip) | (other == sibling))
        def _():
            send_to(step // ahead, other)

        return carry

    in_time = chip < chips // 2
    lax.fori_loop(0, jnp.where(in_time, 2, 1) * ahead, send_before, 0)

    lax.fori_loop(first_tiles, tiles, pack, 0)

    for copy in small[3:]:
        copy.wait()
    wanted = k_ref[0] ^ j_ref[0]
    w_copy.wait()

    def turn(t, carry):
        rows = pl.ds(pl.multiple_of(t * TILE, TILE), TILE)
        for b in range(tiles):
            tile = w_vm[rows, b * TILE : (b + 1) * TILE].astype(jnp.float32)
            tile = jnp.where(tile_ref[t] ^ irreps[b] == wanted, tile, 0.0)
            tile = tile.reshape(group, 2, 8, TILE)
            tile = jnp.concatenate([tile[:, n].reshape(HALF, TILE) for n in range(2)], axis=0)
            wt_vm[b * TILE : (b + 1) * TILE, rows] = tile.T.astype(jnp.bfloat16)
        return carry

    lax.fori_loop(0, tiles, turn, 0)

    a_start = me_p * a_width
    b_start = me_r * b_width
    run_wanted = j_ref[0] ^ tile_ref[a_start // TILE] ^ tile_ref[b_start // TILE]
    met = [i_ref[g * run_len] == run_wanted for g in range(RUNS)]
    row = lax.broadcasted_iota(jnp.int32, (a_width, TILE), 0)
    col = lax.broadcasted_iota(jnp.int32, (a_width, TILE), 1)
    a_row = vir_vm[pl.ds(a_start // TILE, 1), :]
    a_energy = jnp.sum(
        jnp.where(col == row + lax.rem(a_start, TILE), a_row, 0.0), axis=1, keepdims=True
    )
    b_row = vir_vm[pl.ds(b_start // TILE, 1), :]
    b_row = jnp.where(lax.rem(b_start, TILE) == 0, b_row, pltpu.roll(b_row, TILE - b_width, 1))
    for i in range(run_len):
        energy = i_energy[i]
        for g in range(1, RUNS):
            energy = jnp.where(met[g], i_energy[g * run_len + i], energy)
        rows = pl.ds(i * a_width, a_width)
        denom_vm[rows] = a_energy + b_row - energy - j_energy[0]

    def send_chip(half, other):
        @pl.when(half == 0)
        def _():
            pl.semaphore_wait(here_sem.at[other], 1)

        send_to(half, other * 2 + core)
        send_to(half, other * 2 + 1 - core)

    def send_after(other, half):
        send_chip(half, other)
        return half

    def send_later(step, half):
        turn = step // 3
        place = lax.rem(step, 3)
        send_chip(half, jnp.where(place == 0, first + turn, chips - 2 * turn - place))
        return half

    @pl.when(is_first)
    def _():
        def send_half(half, carry):
            lax.fori_loop(chip + 1, first, send_after, half)
            lax.fori_loop(0, chips - first, send_later, half)
            return carry

        lax.fori_loop(0, 2, send_half, 0)

    @pl.when(core == 1)
    def _():
        greeted = 1 + 2 * (rep_count - 1)
        pl.semaphore_wait(
            barrier, jnp.where(is_first, greeted, greeted + 2 * (chips - first - 1))
        )
        pl.semaphore_signal(ok_sem, inc=1, device_id={"blk": sibling}, device_id_type=MESH)

    @pl.when(core == 0)
    def _():
        pl.semaphore_wait(ok_sem, 1)

    def send_last(step, half):
        place = jnp.where(lax.rem(step, 2) == 0, step // 2, blk_count - 2 - step // 2)
        ring = place // 2
        far = chips // 2 - (ring + 1) // 2
        shift = jnp.where(ring % 2 == 1, far, chips - far)
        other = lax.rem(chip + shift, chips) * 2 + lax.rem(me_p + 1 + place, 2)

        @pl.when((other >= 2 * AHEAD) & (step < blk_count - 1))
        def _():
            send_to(half, other)

        turn = step // EVERY

        @pl.when((half == 0) & (lax.rem(step, EVERY) == EVERY - 1) & (turn < 2 * AHEAD) & jnp.logical_not(in_time))
        def _():
            send_to(1, turn)

        return half

    @pl.when(jnp.logical_not(is_first))
    def _():
        def send_half(half, carry):
            lax.fori_loop(0, blk_count, send_last, half)
            return carry

        lax.fori_loop(0, 2, send_half, 0)

    for half in range(2):
        recv[half, me_p] = send[half, me_p]

    others = pl.ds(0, blk_count - 1)
    wide_low = lax.broadcasted_iota(jnp.int32, (b_width // 2, TILE), 1) < HALF
    side = 4
    lines = side * b_width

    def block_at(step):
        ahead_by = jnp.where(step == 0, 2, jnp.where(step == 1, 1, jnp.where(step == 2, 3, 0)))
        return lax.rem(me_r // side + ahead_by, side)

    def send_rep(step, half):
        other = block_at(step // side) * side + lax.rem(me_r + step, side)

        @pl.when(other != me_r)
        def _():
            pltpu.make_async_remote_copy(
                src_ref=part_send.at[half, other],
                dst_ref=part_recv.at[half, me_r],
                send_sem=part_send_sem.at[half],
                recv_sem=part_recv_sem.at[half],
                device_id={"rep": other},
                device_id_type=MESH,
            ).start()

        return half

    for half in range(2):
        pltpu.make_async_copy(
            send.at[half, others], recv.at[half, others], recv_sem.at[half]
        ).wait()
        pieces = []
        for t in range(tiles):
            piece = recv[half, t * group : (t + 1) * group].astype(jnp.float32)
            piece = piece.reshape(HALF, TILE)
            pieces += [piece, pltpu.roll(piece, HALF, 1)]
        left_vm[...] = jnp.concatenate(pieces, axis=0).astype(jnp.bfloat16)

        def reduce(step, carry, half=half):
            block = block_at(step)
            rows = pl.ds(pl.multiple_of(block * lines, lines), lines)
            part = jnp.dot(wt_vm[rows, :], left_vm[...], preferred_element_type=jnp.float32)
            for n in range(side):
                above = part[n * b_width : n * b_width + b_width // 2]
                below = part[n * b_width + b_width // 2 : (n + 1) * b_width]
                part_send[half, block * side + n] = jnp.where(
                    wide_low, above, pltpu.roll(below, HALF, 1)
                )
            lax.fori_loop(step * side, (step + 1) * side, send_rep, half)
            return carry

        lax.fori_loop(0, side, reduce, 0)
        part_recv[half, me_r] = part_send[half, me_r]
    peers = pl.ds(0, rep_count - 1)
    totals = []
    for half in range(2):
        pltpu.make_async_copy(
            part_send.at[half, peers], part_recv.at[half, peers], part_recv_sem.at[half]
        ).wait()
        total = part_recv[half, 0]
        for r in range(1, rep_count):
            total = total + part_recv[half, r]
        totals.append(total)
    above = jnp.where(wide_low, totals[0], pltpu.roll(totals[1], HALF, 1))
    below = jnp.where(wide_low, pltpu.roll(totals[0], HALF, 1), totals[1])
    value = jnp.concatenate([above, below], axis=0).T / denom_vm[:, :b_width]
    for i in range(run_len):
        block = value[i * a_width : (i + 1) * a_width]
        for g in range(RUNS):
            out_ref[g * run_len + i] = jnp.where(met[g], block, 0.0)
    for half in range(2):
        pltpu.make_async_copy(
            send.at[half, others], recv.at[half, others], send_sem.at[half]
        ).wait()
        pltpu.make_async_copy(
            part_send.at[half, peers], part_recv.at[half, peers], part_send_sem.at[half]
        ).wait()


def shards(t_slab, w_cycle, k_irrep, i_irrep, j_irrep, tile_irrep, i_energy, j_energy, vir_energy):
    blk_count = lax.axis_size("blk")
    rep_count = lax.axis_size("rep")
    _, c_width, rows_i, full = t_slab.shape
    tiles = full // TILE
    run_len = rows_i // RUNS
    a_width = full // blk_count
    b_width = full // rep_count
    packed = run_len * a_width
    hbm = pl.BlockSpec(memory_space=pltpu.HBM)
    held = functools.partial(pltpu.with_memory_space_constraint, memory_space=pltpu.HBM)
    result = pl.pallas_call(
        functools.partial(kernel, blk_count, rep_count),
        out_shape=jax.ShapeDtypeStruct((rows_i, a_width, b_width), jnp.float32),
        in_specs=[hbm] * 9,
        out_specs=pl.BlockSpec(memory_space=pltpu.VMEM),
        scratch_shapes=[
            pltpu.SMEM((1,), jnp.int32),
            pltpu.SMEM((rows_i,), jnp.int32),
            pltpu.SMEM((1,), jnp.int32),
            pltpu.SMEM((tiles,), jnp.int32),
            pltpu.SMEM((rows_i,), jnp.float32),
            pltpu.SMEM((1,), jnp.float32),
            pltpu.VMEM((tiles, TILE), jnp.float32),
            pltpu.VMEM((tiles, c_width, rows_i, TILE), jnp.bfloat16),
            pltpu.VMEM((full, full), jnp.bfloat16),
            pltpu.VMEM((full, full), jnp.bfloat16),
            pltpu.VMEM((packed, TILE), jnp.float32),
            pltpu.VMEM((full, packed), jnp.bfloat16),
            pltpu.VMEM((2, blk_count, c_width // 2, packed), jnp.bfloat16),
            pltpu.VMEM((2, blk_count, c_width // 2, packed), jnp.bfloat16),
            pltpu.VMEM((2, rep_count, b_width // 2, packed), jnp.float32),
            pltpu.VMEM((2, rep_count, b_width // 2, packed), jnp.float32),
            pltpu.SemaphoreType.DMA((7,)),
            pltpu.SemaphoreType.DMA((tiles,)),
            pltpu.SemaphoreType.DMA,
            pltpu.SemaphoreType.REGULAR,
            pltpu.SemaphoreType.REGULAR((blk_count // 2,)),
            pltpu.SemaphoreType.DMA((2,)),
            pltpu.SemaphoreType.DMA((2,)),
            pltpu.SemaphoreType.DMA((2,)),
            pltpu.SemaphoreType.DMA((2,)),
        ],
        compiler_params=pltpu.CompilerParams(
            collective_id=0, has_side_effects=True, vmem_limit_bytes=40 * 2**20
        ),
    )(
        k_irrep,
        held(i_irrep),
        j_irrep,
        held(tile_irrep),
        held(i_energy),
        j_energy,
        held(vir_energy.reshape(tiles, TILE)),
        held(t_slab[0]),
        held(w_cycle[0, 0]),
    )
    return result[None]


def solution(mesh):
    in_specs = (
        P("rep", "blk", None, None),
        P("rep", None, None, None),
        P("rep"),
        P(),
        P(),
        P(),
        P(),
        P(),
        P(),
    )
    out_specs = P(None, None, "blk", "rep")
    return jax.shard_map(shards, mesh=mesh, in_specs=in_specs, out_specs=out_specs, check_vma=False)
```
